512 devices in a mesh: seg: 16 (over y, core), blk: 32 (over z, x).
Axes of the slice: x: 4, y: 8, z: 8, core: 2. Of those that a mesh axis runs over, the one named last changes fastest.
Arguments:
- site: bfloat16 [16, 32, 128, 512], P('seg', 'blk'), may hold values from -6 to 6
- left_env: bfloat16 [16, 30, 32, 128, 128], P('seg', None, 'blk'), may hold values from -2 to 5
- right_env: bfloat16 [16, 30, 32, 128, 128], P('seg', None, 'blk'), may hold values from -2 to 5
- mpo: float32 [30, 4, 4], replicated, may hold values from -2 to 5
- channel_charge: int32 [30], replicated, may hold values from -1 to 1
- kept: int32 [16, 32], P('seg', 'blk'), may hold values from 1 to 128, 3072 in all within a row
Outputs:
- site_out: bfloat16 [16, 32, 128, 512], P('seg', 'blk')
- energy: float32 [16], P('seg')
- merged_env: bfloat16 [16, 30, 32, 128, 128], P('seg', None, 'blk')
The draws below stay inside these ranges and needn't reach their ends.
Inputs may be any that keep to these rules, and one draw needn't show every extreme that they name: In each segment the kept dimensions sum to 3072 and the largest equals 128.
All inputs are finite; a program needn't handle non-finite values. No bound on the sum of `kept` on one device may be relied on, other than what follows from the above.
Results may differ from the reference program's by a relative error of at most 0.012.
Values may be sent and summed in bfloat16 or wider, within the bound.
No kernel may reach another device: no remote copies, remote signals or barrier semaphores. Data moves between devices by JAX's collectives and lax.ppermute only.
A program may use at most 64 MiB of HBM per device.

```python
import math
import jax
import jax.numpy as jnp
import numpy as np
from jax import lax

BLK = 128
PHYS = 4
W = 30
ITERS = 3
NSEC = 32
NSEG = 16


def env_blocks(key, noise_std, sec_lo, sec_hi, chan_lo, chan_hi):
    eye = jnp.eye(BLK, dtype=jnp.float32)

    def one_segment(index):
        seg_key = jax.random.fold_in(key, index)
        knoise, ksector, kchannel = jax.random.split(seg_key, 3)
        raw = jnp.clip(jax.random.normal(knoise, (W, NSEC, BLK, BLK), jnp.float32), -6.0, 6.0)
        noise = (raw + jnp.swapaxes(raw, -1, -2)) * (noise_std * math.sqrt(0.5))
        sector = jnp.exp(jax.random.uniform(ksector, (1, NSEC), jnp.float32, math.log(sec_lo), math.log(sec_hi)))
        channel = jax.random.uniform(kchannel, (W, NSEC), jnp.float32, chan_lo, chan_hi)
        shift = sector * channel
        return (noise + shift[:, :, None, None] * eye).astype(jnp.bfloat16)
    return lax.map(one_segment, jnp.arange(NSEG, dtype=jnp.int32))


def draw_left_env(key, part):
    key = jax.random.fold_in(key, 11)
    return env_blocks(key, 0.5 / math.sqrt(BLK), 0.6, 1.6, 0.7, 1.3)


def draw_right_env(key, part):
    key = jax.random.fold_in(key, 12)
    return env_blocks(key, 0.5 / math.sqrt(BLK), 0.6, 1.6, 0.7, 1.3)


def channel_ops(key, noise_std, diag_lo, diag_hi):
    knoise, kdiag = jax.random.split(key, 2)
    raw = jnp.clip(jax.random.normal(knoise, (W, PHYS, PHYS), jnp.float32), -6.0, 6.0)
    noise = (raw + jnp.swapaxes(raw, -1, -2)) * (noise_std * math.sqrt(0.5))
    diag = jax.random.uniform(kdiag, (W,), jnp.float32, diag_lo, diag_hi) / W
    return noise + diag[:, None, None] * jnp.eye(PHYS, dtype=jnp.float32)


def draw_mpo(key, part):
    key = jax.random.fold_in(key, 13)
    return channel_ops(key, 1.0 / math.sqrt(W * PHYS), 2.0, 10.0)


def touch_ends(array, own_key, low, largest):
    index_at = [jax.random.randint(jax.random.fold_in(own_key, axis), (), 0, length) for axis, length in enumerate(array.shape)]
    longest = array.shape.index(max(array.shape))
    beside = index_at[:longest] + [(index_at[longest] + 1) % array.shape[longest]] + index_at[longest + 1:]
    return array.at[tuple(index_at)].set(low).at[tuple(beside)].set(largest)


def shard_levels(stream_key, dims, cuts, smallest, high):
    gain, own = 1.0, jax.random.fold_in(stream_key, 6)
    for position, shards_of in cuts:
        steps = jnp.exp(jax.random.uniform(jax.random.fold_in(own, position), (shards_of,), jnp.float32, smallest / len(cuts), high / len(cuts)))
        gain = gain * jnp.repeat(steps, dims[position] // shards_of).reshape([-1 if axis == position else 1 for axis in range(len(dims))])
    return gain


def length_profile(number_of, total, reach, skew):
    weights = [(1 << 20) // math.isqrt(standing ** skew) + 1 for standing in range(2, number_of + 1)]
    spare, counts = total - reach - (number_of - 1), [1] * (number_of - 1)
    while spare > 0:
        candidates = [i for i in range(number_of - 1) if counts[i] < reach]
        mass, budget = sum([weights[i] for i in candidates]), spare
        for i in candidates:
            addition = min(reach - counts[i], max(1, budget * weights[i] // mass), spare)
            counts[i] = counts[i] + addition
            spare = spare - addition
    return np.array([reach] + counts)


def uneven(key, count, total, bound, lean):
    if count == 2:
        one = jax.random.randint(key, (), max(1, total - bound), min(bound, total - 1) + 1)
        return jnp.stack([one, total - one])
    sizes = jnp.asarray(length_profile(count, total, bound, lean), jnp.int32)
    pairs = (count - 1) // 2
    source_of, taker = sizes[1:1 + 2 * pairs:2], sizes[2:2 + 2 * pairs:2]
    room = jnp.minimum(source_of - 1, bound - taker)
    shifted = jax.random.randint(jax.random.fold_in(key, 1), (pairs,), 0, 1 << 20) % (room + 1)
    sizes = sizes.at[1:1 + 2 * pairs:2].set(source_of - shifted).at[2:2 + 2 * pairs:2].set(taker + shifted)
    return sizes[jax.random.permutation(jax.random.fold_in(key, 2), count)]


def normal_values(rng, dims, width, bound, shards=(), kind=jnp.bfloat16):
    values = jax.random.normal(rng, dims, jnp.float32) * width
    if len(shards) > 0:
        values = shard_levels(rng, dims, shards, -0.22, 0.18) * values
    return jnp.clip(values, min=-bound, max=bound).astype(kind)


def setup_inputs(seed: int = 0) -> dict:
    seeds = jax.random.split(jax.random.key(seed), 7)
    return {
        "site": normal_values(seeds[0], (NSEG, NSEC, BLK, PHYS * BLK), 1.0, 6.0, ((0, 16), (1, 32))),
        "left_env": draw_left_env(jax.random.fold_in(seeds[6], 71), 0),
        "right_env": draw_right_env(jax.random.fold_in(seeds[6], 71), 0),
        "mpo": draw_mpo(jax.random.fold_in(seeds[6], 71), 0),
        "channel_charge": touch_ends(jax.random.randint(seeds[4], (W,), -1, 2), jax.random.fold_in(seeds[4], 1), -1, 1).astype(jnp.int32),
        "kept": jax.vmap(lambda own: uneven(own, NSEC, 3 * NSEC * BLK // 4, BLK, 1))(jax.random.split(seeds[5], NSEG)).reshape((NSEG, NSEC)).astype(jnp.int32),
    }


def coef_table(channel_charge, mpo):
    pick = (jnp.arange(3)[None, :] == (1 - channel_charge)[:, None]).astype(jnp.float32)
    return pick[:, :, None, None] * mpo[:, None, :, :]

def channel_terms(ext3, lblock, coef):
    extf = ext3.astype(jnp.float32).reshape(3, BLK, PHYS, BLK)
    tsel = jnp.zeros((W, BLK, PHYS, BLK), jnp.float32)
    for offset in range(3):
        for column in range(PHYS):
            tsel = tsel + coef[:, offset, :, column][:, None, :, None] * extf[offset, :, column, :][None, :, None, :]
    tsel = tsel.astype(jnp.bfloat16).reshape(W, BLK, PHYS * BLK)
    mixed = jnp.einsum('alm,amn->aln', lblock.astype(jnp.float32), tsel.astype(jnp.float32))
    return mixed.astype(jnp.bfloat16).reshape(W, BLK, PHYS, BLK)

def make_mask(kept_seg):
    rows = jnp.arange(BLK)
    cols = jnp.arange(PHYS * BLK) % BLK
    return (rows[None, :, None] < kept_seg[:, None, None]) & (cols[None, None, :] < kept_seg[:, None, None])

def apply_ham(x, lseg, rseg, coef):
    padded = jnp.pad(x, ((1, 1), (0, 0), (0, 0)))

    def single(sector):
        ext3 = lax.dynamic_slice_in_dim(padded, sector, 3, 0)
        lblock = lax.dynamic_index_in_dim(lseg, sector, 1, keepdims=False)
        rblock = lax.dynamic_index_in_dim(rseg, sector, 1, keepdims=False)
        mixed = channel_terms(ext3, lblock, coef)
        out = jnp.einsum('alir,art->lit', mixed.astype(jnp.float32), rblock.astype(jnp.float32))
        return out.reshape(BLK, PHYS * BLK)
    return lax.map(single, jnp.arange(NSEC, dtype=jnp.int32))

def segment_env(x, lseg, coef):
    padded = jnp.pad(x, ((1, 1), (0, 0), (0, 0)))
    factor = jnp.float32(NSEC * BLK * BLK)

    def single(sector):
        ext3 = lax.dynamic_slice_in_dim(padded, sector, 3, 0)
        lblock = lax.dynamic_index_in_dim(lseg, sector, 1, keepdims=False)
        mixed = channel_terms(ext3, lblock, coef)
        block = lax.dynamic_index_in_dim(x, sector, 0, keepdims=False).reshape(BLK, PHYS, BLK)
        total = jnp.einsum('lir,alis->ars', block.astype(jnp.float32), mixed.astype(jnp.float32))
        return (factor * total).astype(jnp.bfloat16)
    return jnp.transpose(lax.map(single, jnp.arange(NSEC, dtype=jnp.int32)), (1, 0, 2, 3))

def segment_solve(site_seg, lseg, rseg, kept_seg, coef):
    mask = make_mask(kept_seg)
    x = jnp.where(mask, site_seg, jnp.zeros_like(site_seg))
    energy = jnp.float32(0.0)
    for step in range(ITERS):
        h = apply_ham(x, lseg, rseg, coef)
        h = jnp.where(mask, h, jnp.zeros_like(h))
        xf = x.astype(jnp.float32)
        rr = jnp.sum(xf * xf)
        xh = jnp.sum(xf * h)
        hh = jnp.sum(h * h)
        energy = xh / rr
        res = h - energy * xf
        rres = jnp.maximum(hh - energy * xh, 0.0)
        x = ((xf - 0.5 * res) / jnp.sqrt(rr + 0.25 * rres)).astype(jnp.bfloat16)
    return (x, energy)

def reference(site, left_env, right_env, mpo, channel_charge, kept):
    coef = coef_table(channel_charge, mpo)
    outs = []
    energies = []
    envs = [left_env[0]]
    for j in range(NSEG):
        x, energy = segment_solve(site[j], left_env[j], right_env[j], kept[j], coef)
        outs.append(x)
        energies.append(energy)
        if j + 1 < NSEG:
            envs.append(segment_env(x, left_env[j], coef))
    return (jnp.stack(outs), jnp.stack(energies), jnp.stack(envs))
```

```python
import functools

import jax
import jax.numpy as jnp
from jax import lax
from jax.experimental import pallas as pl
from jax.experimental.pallas import tpu as pltpu
from jax.sharding import PartitionSpec as P

ITERS = 3
SHRINK = 2.0**-12
VMEM_LIMIT = 48 << 20

SMEM_SPEC = pl.BlockSpec(memory_space=pltpu.SMEM)
VMEM_SPEC = pl.BlockSpec(memory_space=pltpu.VMEM)


def kernel_call(body, out_shape, out_specs, in_specs, name, scratch=()):
    return pl.pallas_call(
        body,
        out_shape=out_shape,
        in_specs=in_specs,
        out_specs=out_specs,
        scratch_shapes=scratch,
        name=name,
        compiler_params=pltpu.CompilerParams(vmem_limit_bytes=VMEM_LIMIT),
    )


def shift_of(mpo_ref, charge_ref, chans, phys):
    total = jnp.float32(0.0)
    for a in range(chans):
        trace = mpo_ref[a * phys * phys]
        for i in range(1, phys):
            trace = trace + mpo_ref[a * phys * phys + i * (phys + 1)]
        total = total + jnp.where(charge_ref[a] == 0, trace, 0.0)
    return 2.0 + total * (1.0 / phys)


def mixed_blocks(a, ext_ref, l_ref, mpo_ref, charge_ref, width, phys):
    product = jnp.dot(l_ref[a], ext_ref[1 - charge_ref[a]], preferred_element_type=jnp.float32)
    blocks = []
    for i in range(phys):
        total = None
        for q in range(phys):
            term = mpo_ref[a * phys * phys + i * phys + q] * product[:, q * width : (q + 1) * width]
            total = term if total is None else total + term
        blocks.append(total.astype(jnp.bfloat16))
    return jnp.concatenate(blocks, axis=0)


def mixed_pair(pair, *rest):
    return jnp.concatenate([mixed_blocks(2 * pair, *rest), mixed_blocks(2 * pair + 1, *rest)], axis=1)


def total_of(values):
    return jnp.sum(jnp.sum(values, axis=0, keepdims=True), axis=1, keepdims=True)


def pairs_of(count):
    return [(a, b) for a in range(count) for b in range(a, count)]


def apply_kernel(chans, width, phys, history, mpo_ref, charge_ref, kept_ref, own_ref, left_ref, right_ref, l_ref, r_ref, *refs):
    earlier = refs[:history]
    outs = refs[history:-1]
    ext_ref = refs[-1]
    own = own_ref[...].astype(jnp.float32)
    ext_ref[0] = left_ref[...]
    ext_ref[1] = own.astype(jnp.bfloat16)
    ext_ref[2] = right_ref[...]
    total = None
    for pair in range(chans // 2):
        lhs = mixed_pair(pair, ext_ref, l_ref, mpo_ref, charge_ref, width, phys)
        term = jnp.dot(lhs, r_ref[pair], preferred_element_type=jnp.float32)
        total = term if total is None else total + term
    kept = kept_ref[0]
    rows = lax.broadcasted_iota(jnp.int32, (width, width), 0)
    cols = lax.broadcasted_iota(jnp.int32, (width, width), 1)
    mask = (rows < kept) & (cols < kept)
    shift = shift_of(mpo_ref, charge_ref, chans, phys)
    parts = []
    for i in range(phys):
        cut = slice(i * width, (i + 1) * width)
        part = SHRINK * (jnp.where(mask, total[cut, :], 0.0) - shift * own[:, cut])
        outs[0][:, cut] = part
        outs[1][:, cut] = part.astype(jnp.bfloat16)
        parts.append(part)
    if history:
        vectors = [ref[...].astype(jnp.float32) for ref in earlier] + [own, jnp.concatenate(parts, axis=1)]
        lane = lax.broadcasted_iota(jnp.int32, (1, width), 1)
        row = jnp.zeros((1, width), jnp.float32)
        for k, (a, b) in enumerate(pairs_of(len(vectors))):
            row = row + jnp.where(lane == k, total_of(vectors[a] * vectors[b]), 0.0)
        outs[2][...] = jnp.broadcast_to(row[None], outs[2].shape)


def apply_ham(own, left, right, lenv, renv, mpo, charge, kept, earlier, peers):
    chans, width, _ = lenv.shape
    phys = own.shape[1] // width
    shapes = [jax.ShapeDtypeStruct(own.shape, jnp.float32), jax.ShapeDtypeStruct(own.shape, jnp.bfloat16)]
    if earlier:
        shapes.append(jax.ShapeDtypeStruct((peers, 1, width), jnp.float32))
    return kernel_call(
        functools.partial(apply_kernel, chans, width, phys, len(earlier)),
        shapes,
        [VMEM_SPEC] * len(shapes),
        [SMEM_SPEC] * 3 + [VMEM_SPEC] * (5 + len(earlier)),
        "apply_ham",
        [pltpu.VMEM((3, *own.shape), jnp.bfloat16)],
    )(mpo, charge, kept, own, left, right, lenv, renv, *earlier)


def combine_kernel(chans, width, phys, mpo_ref, charge_ref, sums_ref, *refs):
    count = ITERS + 1
    own, left, right = refs[:count], refs[count : 2 * count], refs[2 * count : 3 * count]
    ext_ref, energy_ref = refs[3 * count :]
    shift = shift_of(mpo_ref, charge_ref, chans, phys)
    row = jnp.sum(sums_ref[...], axis=0)
    lane = lax.broadcasted_iota(jnp.int32, row.shape, 1)
    gram = {}
    for k, (a, b) in enumerate(pairs_of(count)):
        gram[a, b] = gram[b, a] = jnp.sum(jnp.where(lane == k, row, 0.0), axis=1, keepdims=True)

    def inner(p, q):
        total = None
        for a, pa in enumerate(p):
            for b, qb in enumerate(q):
                term = gram[a, b] * (pa * qb)
                total = term if total is None else total + term
        return total

    p = [jnp.ones((1, 1), jnp.float32)]
    energy = None
    for _ in range(ITERS):
        hp = [shift * c for c in p] + [jnp.zeros((1, 1), jnp.float32)]
        for k, c in enumerate(p):
            hp[k + 1] = hp[k + 1] + (1.0 / SHRINK) * c
        rr, xh, hh = inner(p, p), inner(p, hp), inner(hp, hp)
        energy = xh / rr
        rres = jnp.maximum(hh - energy * xh, 0.0)
        scale = 1.0 / jnp.sqrt(rr + 0.25 * rres)
        grown = p + [jnp.zeros((1, 1), jnp.float32)]
        p = [scale * (c - 0.5 * (h - energy * c)) for c, h in zip(grown, hp)]
    for place, vectors in enumerate((left, own, right)):
        x = None
        for c, ref in zip(p, vectors):
            term = c * ref[...].astype(jnp.float32)
            x = term if x is None else x + term
        ext_ref[place] = x.astype(jnp.bfloat16)
    energy_ref[...] = jnp.broadcast_to(energy, energy_ref.shape)


def combine(own, left, right, sums, mpo, charge, chans, width):
    phys = own[0].shape[1] // width
    return kernel_call(
        functools.partial(combine_kernel, chans, width, phys),
        [jax.ShapeDtypeStruct((3, *own[0].shape), jnp.bfloat16), jax.ShapeDtypeStruct((1, width), jnp.float32)],
        [VMEM_SPEC] * 2,
        [SMEM_SPEC] * 2 + [VMEM_SPEC] * (1 + 3 * len(own)),
        "combine",
    )(mpo, charge, sums, *own, *left, *right)


def env_kernel(chans, width, phys, factor, mpo_ref, charge_ref, first_ref, ext_ref, l_ref, own_l_ref, out_ref):
    @pl.when(first_ref[0] != 0)
    def _():
        out_ref[...] = own_l_ref[...]

    @pl.when(first_ref[0] == 0)
    def _():
        x = ext_ref[1].astype(jnp.float32)
        turned = jnp.concatenate(
            [x[:, i * width : (i + 1) * width].T.astype(jnp.bfloat16) for i in range(phys)], axis=1
        )
        for pair in range(chans // 2):
            rhs = mixed_pair(pair, ext_ref, l_ref, mpo_ref, charge_ref, width, phys)
            total = jnp.dot(turned, rhs, preferred_element_type=jnp.float32)
            for k in range(2):
                out_ref[2 * pair + k] = (factor * total[:, k * width : (k + 1) * width]).astype(jnp.bfloat16)


def env_of(ext, lprev, lenv, mpo, charge, first, factor):
    chans, width, _ = lenv.shape
    phys = ext.shape[2] // width
    return kernel_call(
        functools.partial(env_kernel, chans, width, phys, factor),
        jax.ShapeDtypeStruct(lenv.shape, jnp.bfloat16),
        VMEM_SPEC,
        [SMEM_SPEC] * 3 + [VMEM_SPEC] * 3,
        "new_env",
    )(mpo, charge, first, ext, lprev, lenv)


def neighbours(x):
    count = lax.axis_size("blk")
    left = lax.ppermute(x, "blk", [(i, i + 1) for i in range(count - 1)])
    right = lax.ppermute(x, "blk", [(i + 1, i) for i in range(count - 1)])
    return left, right


def passed_along(array):
    length = lax.axis_size("seg")
    return lax.ppermute(array, "seg", [(i, i + 1) for i in range(length - 1)])


def on_device(site, left_env, right_env, mpo, channel_charge, kept):
    width = site.shape[2]
    cols_all = site.shape[3]
    chans = left_env.shape[1]
    peers = lax.axis_size("blk")
    factor = float(site.shape[1] * peers * width * width)
    lenv = left_env[0, :, 0]
    renv = right_env[0, :, 0].reshape(chans // 2, 2 * width, width)
    mpo = mpo.reshape(-1)
    limit = kept[0]
    rows = jnp.arange(width)
    cols = jnp.arange(cols_all) % width
    mask = (rows[:, None] < limit) & (cols[None, :] < limit)
    x = jnp.where(mask, site[0, 0], jnp.zeros_like(site[0, 0]))
    lprev = passed_along(lenv)
    own, left, right = [x], [], []
    rounded = x
    sums = None
    for step in range(ITERS):
        from_left, from_right = neighbours(rounded)
        left.append(from_left)
        right.append(from_right)
        earlier = own[:-1] if step == ITERS - 1 else []
        nxt, rounded, *sums = apply_ham(
            own[-1], from_left, from_right, lenv, renv, mpo, channel_charge, limit, earlier, peers
        )
        own.append(nxt)
    from_left, from_right = neighbours(rounded)
    left.append(from_left)
    right.append(from_right)
    sums = lax.all_to_all(sums[0], "blk", 0, 0)
    ext, energy = combine(own, left, right, sums, mpo, channel_charge, chans, width)
    arrived = passed_along(ext)
    first = (lax.axis_index("seg") == 0).astype(jnp.int32).reshape(1)
    merged = env_of(arrived, lprev, lenv, mpo, channel_charge, first, factor)
    return ext[1][None, None], energy[0, :1], merged[None, :, None]


def solution(mesh):
    placed = (
        P("seg", "blk", None, None),
        P("seg", None, "blk", None, None),
        P("seg", None, "blk", None, None),
        P(),
        P(),
        P("seg", "blk"),
    )
    return jax.shard_map(
        on_device,
        mesh=mesh,
        in_specs=placed,
        out_specs=(P("seg", "blk", None, None), P("seg"), P("seg", None, "blk", None, None)),
        check_vma=False,
    )
```

```python
import functools

import jax
import jax.numpy as jnp
from jax import lax
from jax.experimental import pallas as pl
from jax.experimental.pallas import tpu as pltpu
from jax.sharding import PartitionSpec as P

ITERS = 3
SHRINK = 2.0**-12
VMEM_LIMIT = 48 << 20
EXTRA = 16
GROUP = 4

SMEM_SPEC = pl.BlockSpec(memory_space=pltpu.SMEM)
VMEM_SPEC = pl.BlockSpec(memory_space=pltpu.VMEM)


def kernel_call(body, out_shape, out_specs, in_specs, name, scratch=()):
    return pl.pallas_call(
        body,
        out_shape=out_shape,
        in_specs=in_specs,
        out_specs=out_specs,
        scratch_shapes=scratch,
        name=name,
        compiler_params=pltpu.CompilerParams(vmem_limit_bytes=VMEM_LIMIT),
    )


def shift_of(mpo_ref, charge_ref, chans, phys):
    total = jnp.float32(0.0)
    for a in range(chans):
        trace = mpo_ref[a * phys * phys]
        for i in range(1, phys):
            trace = trace + mpo_ref[a * phys * phys + i * (phys + 1)]
        total = total + jnp.where(charge_ref[a] == 0, trace, 0.0)
    return 2.0 + total * (1.0 / phys)


def mixed_blocks(a, ext_ref, l_ref, mpo_ref, charge_ref, width, phys):
    product = jnp.dot(l_ref[a], ext_ref[1 - charge_ref[a]], preferred_element_type=jnp.float32)
    blocks = []
    for i in range(phys):
        total = None
        for q in range(phys):
            term = mpo_ref[a * phys * phys + i * phys + q] * product[:, q * width : (q + 1) * width]
            total = term if total is None else total + term
        blocks.append(total.astype(jnp.bfloat16))
    return jnp.concatenate(blocks, axis=0)


def mixed_group(chosen, *rest):
    return jnp.concatenate([mixed_blocks(a, *rest) for a in chosen], axis=1)


def set_neighbours(ext_ref, odd, inner, outer):
    ext_ref[2 - 2 * odd] = inner
    ext_ref[2 * odd] = outer[: inner.shape[0]]


def total_of(values):
    return jnp.sum(jnp.sum(values, axis=0, keepdims=True), axis=1, keepdims=True)


def pairs_of(count):
    return [(a, b) for a in range(count) for b in range(a, count)]


def apply_kernel(chans, width, phys, history, mpo_ref, charge_ref, kept_ref, odd_ref, own_ref, inner_ref, outer_ref, l_ref, r_ref, *refs):
    earlier = refs[:history]
    outs = refs[history:-1]
    ext_ref = refs[-1]
    own = own_ref[...].astype(jnp.float32)
    ext_ref[1] = own.astype(jnp.bfloat16)
    set_neighbours(ext_ref, odd_ref[0], inner_ref[...], outer_ref[...])
    total = None
    for first in range(0, chans, GROUP):
        chosen = range(first, min(first + GROUP, chans))
        lhs = mixed_group(chosen, ext_ref, l_ref, mpo_ref, charge_ref, width, phys)
        rhs = r_ref[first : first + len(chosen)].reshape(len(chosen) * width, width)
        term = jnp.dot(lhs, rhs, preferred_element_type=jnp.float32)
        total = term if total is None else total + term
    kept = kept_ref[0]
    rows = lax.broadcasted_iota(jnp.int32, (width, width), 0)
    cols = lax.broadcasted_iota(jnp.int32, (width, width), 1)
    mask = (rows < kept) & (cols < kept)
    shift = shift_of(mpo_ref, charge_ref, chans, phys)
    parts = []
    for i in range(phys):
        cut = slice(i * width, (i + 1) * width)
        part = SHRINK * (jnp.where(mask, total[cut, :], 0.0) - shift * own[:, cut])
        outs[0][:, cut] = part
        outs[1][:, cut] = part.astype(jnp.bfloat16)
        outs[2][:width, cut] = part.astype(jnp.bfloat16)
        parts.append(part)
    outs[2][width:, :] = jnp.zeros((EXTRA, own.shape[1]), jnp.bfloat16)
    if history:
        vectors = [ref[...].astype(jnp.float32) for ref in earlier] + [own, jnp.concatenate(parts, axis=1)]
        lane = lax.broadcasted_iota(jnp.int32, (1, width), 1)
        row = jnp.zeros((1, width), jnp.float32)
        for k, (a, b) in enumerate(pairs_of(len(vectors))):
            row = row + jnp.where(lane == k, total_of(vectors[a] * vectors[b]), 0.0)
        outs[3][...] = jnp.broadcast_to(row[None], outs[3].shape)


def sent_shapes(shape):
    rows, cols = shape
    return [jax.ShapeDtypeStruct((size, cols), jnp.bfloat16) for size in (rows, rows + EXTRA)]


def apply_ham(own, inner, outer, lenv, renv, mpo, charge, kept, odd, earlier, peers):
    chans, width, _ = lenv.shape
    phys = own.shape[1] // width
    shapes = [jax.ShapeDtypeStruct(own.shape, jnp.float32), *sent_shapes(own.shape)]
    if earlier:
        shapes.append(jax.ShapeDtypeStruct((peers, 1, width), jnp.float32))
    return kernel_call(
        functools.partial(apply_kernel, chans, width, phys, len(earlier)),
        shapes,
        [VMEM_SPEC] * len(shapes),
        [SMEM_SPEC] * 4 + [VMEM_SPEC] * (5 + len(earlier)),
        "apply_ham",
        [pltpu.VMEM((3, *own.shape), jnp.bfloat16)],
    )(mpo, charge, kept, odd, own, inner, outer, lenv, renv, *earlier)


def combine_kernel(chans, phys, mpo_ref, charge_ref, odd_ref, sums_ref, *refs):
    count = ITERS + 1
    own, inner_refs, outer_refs = refs[:count], refs[count : 2 * count], refs[2 * count : 3 * count]
    ext_ref, energy_ref = refs[3 * count :]
    shift = shift_of(mpo_ref, charge_ref, chans, phys)
    row = jnp.sum(sums_ref[...], axis=0)
    lane = lax.broadcasted_iota(jnp.int32, row.shape, 1)
    gram = {}
    for k, (a, b) in enumerate(pairs_of(count)):
        gram[a, b] = gram[b, a] = jnp.sum(jnp.where(lane == k, row, 0.0), axis=1, keepdims=True)

    def product(p, q):
        total = None
        for a, pa in enumerate(p):
            for b, qb in enumerate(q):
                term = gram[a, b] * (pa * qb)
                total = term if total is None else total + term
        return total

    p = [jnp.ones((1, 1), jnp.float32)]
    energy = None
    for _ in range(ITERS):
        hp = [shift * c for c in p] + [jnp.zeros((1, 1), jnp.float32)]
        for k, c in enumerate(p):
            hp[k + 1] = hp[k + 1] + (1.0 / SHRINK) * c
        rr, xh, hh = product(p, p), product(p, hp), product(hp, hp)
        energy = xh / rr
        rres = jnp.maximum(hh - energy * xh, 0.0)
        scale = 1.0 / jnp.sqrt(rr + 0.25 * rres)
        grown = p + [jnp.zeros((1, 1), jnp.float32)]
        p = [scale * (c - 0.5 * (h - energy * c)) for c, h in zip(grown, hp)]
    def final(vectors):
        x = None
        for c, ref in zip(p, vectors):
            term = c * ref[: ext_ref.shape[1]].astype(jnp.float32)
            x = term if x is None else x + term
        return x.astype(jnp.bfloat16)

    ext_ref[1] = final(own)
    set_neighbours(ext_ref, odd_ref[0], final(inner_refs), final(outer_refs))
    energy_ref[...] = jnp.broadcast_to(energy, energy_ref.shape)


def combine(own, inner, outer, sums, mpo, charge, odd, chans, width):
    phys = own[0].shape[1] // width
    return kernel_call(
        functools.partial(combine_kernel, chans, phys),
        [jax.ShapeDtypeStruct((3, *own[0].shape), jnp.bfloat16), jax.ShapeDtypeStruct((8, width), jnp.float32)],
        [VMEM_SPEC] * 2,
        [SMEM_SPEC] * 3 + [VMEM_SPEC] * (1 + 3 * len(own)),
        "combine",
    )(mpo, charge, odd, sums, *own, *inner, *outer)


def env_kernel(chans, width, phys, factor, mpo_ref, charge_ref, first_ref, ext_ref, l_ref, own_l_ref, out_ref, cols_ref, turned_ref, made_ref, sems):
    parts = [pl.ds(2 * pair, 2) for pair in range(chans // 2)]

    @pl.when(first_ref[0] != 0)
    def _():
        copy = pltpu.make_async_copy(own_l_ref, out_ref, sems.at[0])
        copy.start()
        copy.wait()

    @pl.when(first_ref[0] == 0)
    def _():
        for i in range(phys):
            cut = slice(i * width, (i + 1) * width)
            for place in range(3):
                cols_ref[place, cut, :] = ext_ref[place, :, cut]
            turned_ref[cut, :] = ext_ref[1, :, cut].astype(jnp.float32).T.astype(jnp.bfloat16)
        copies = []
        for pair, part in enumerate(parts):
            both = jnp.concatenate([l_ref[2 * pair], l_ref[2 * pair + 1]], axis=1)
            left = jnp.dot(turned_ref[...], both, preferred_element_type=jnp.float32)
            for k in range(2):
                a = 2 * pair + k
                blocks = []
                for q in range(phys):
                    total = None
                    for i in range(phys):
                        cut = left[i * width : (i + 1) * width, k * width : (k + 1) * width]
                        term = mpo_ref[a * phys * phys + i * phys + q] * cut
                        total = term if total is None else total + term
                    blocks.append(total.astype(jnp.bfloat16))
                made = jnp.dot(
                    jnp.concatenate(blocks, axis=1), cols_ref[1 - charge_ref[a]], preferred_element_type=jnp.float32
                )
                made_ref[a] = (factor * made).astype(jnp.bfloat16)
            copies.append(pltpu.make_async_copy(made_ref.at[part], out_ref.at[part], sems.at[pair]))
            copies[-1].start()
        for copy in copies:
            copy.wait()


def env_of(ext, lprev, lenv, mpo, charge, first, factor):
    chans, width, _ = lenv.shape
    phys = ext.shape[2] // width
    return kernel_call(
        functools.partial(env_kernel, chans, width, phys, factor),
        jax.ShapeDtypeStruct(lenv.shape, jnp.bfloat16),
        pl.BlockSpec(memory_space=pl.ANY),
        [SMEM_SPEC] * 3 + [VMEM_SPEC] * 3,
        "new_env",
        [
            pltpu.VMEM((3, phys * width, width), jnp.bfloat16),
            pltpu.VMEM((phys * width, width), jnp.bfloat16),
            pltpu.VMEM(lenv.shape, jnp.bfloat16),
            pltpu.SemaphoreType.DMA((chans // 2,)),
        ],
    )(mpo, charge, first, ext, lprev, lenv)


def hold_kernel(*refs):
    pass


def held_in_vmem(lenv, renv, charge, mpo):
    return pl.pallas_call(
        hold_kernel,
        out_shape=[jax.ShapeDtypeStruct(array.shape, array.dtype) for array in (lenv, renv)],
        in_specs=[VMEM_SPEC] * 2 + [SMEM_SPEC] * 2,
        out_specs=[VMEM_SPEC] * 2,
        input_output_aliases={0: 0, 1: 1},
        name="hold",
        compiler_params=pltpu.CompilerParams(vmem_limit_bytes=VMEM_LIMIT),
    )(lenv, renv, charge, mpo)


def mask_kernel(width, kept_ref, site_ref, out_ref, long_ref):
    kept = kept_ref[0]
    rows = lax.broadcasted_iota(jnp.int32, site_ref.shape, 0)
    cols = lax.broadcasted_iota(jnp.int32, site_ref.shape, 1) % width
    site = site_ref[...].astype(jnp.float32)
    site = jnp.where((rows < kept) & (cols < kept), site, 0.0).astype(jnp.bfloat16)
    out_ref[...] = site
    long_ref[:width] = site
    long_ref[width:] = jnp.zeros((EXTRA, site.shape[1]), jnp.bfloat16)


def masked(site, kept):
    width = site.shape[0]
    return kernel_call(
        functools.partial(mask_kernel, width),
        sent_shapes(site.shape),
        [VMEM_SPEC] * 2,
        [SMEM_SPEC, VMEM_SPEC],
        "masked",
    )(kept, site)


def neighbours(x, long):
    count = lax.axis_size("blk")
    outer = lax.ppermute(long, "blk", [(i, i + 1 if i % 2 else i - 1) for i in range(1, count - 1)])
    inner = lax.ppermute(x, "blk", [(i, i ^ 1) for i in range(count)])
    return inner, outer


def passed_along(array):
    length = lax.axis_size("seg")
    return lax.ppermute(array, "seg", [(i, i + 1) for i in range(length - 1)])


def on_device(site, left_env, right_env, mpo, charge, kept):
    width = site.shape[2]
    chans = left_env.shape[1]
    peers = lax.axis_size("blk")
    factor = float(site.shape[1] * peers * width * width)
    lenv = left_env[0, :, 0]
    renv = right_env[0, :, 0]
    mpo = mpo.reshape(-1)
    limit = kept[0]
    x, long = masked(site[0, 0], limit)
    held = lax.optimization_barrier((x, lenv, renv))
    lheld, rheld = held_in_vmem(*held[1:], charge, mpo)
    odd = (lax.axis_index("blk") % 2).astype(jnp.int32).reshape(1)
    own, inner, outer = [x], [], []
    rounded = x
    for step in range(ITERS):
        from_inner, from_outer = neighbours(rounded, long)
        inner.append(from_inner)
        outer.append(from_outer)
        if step == 0:
            from_inner, from_outer, later = lax.optimization_barrier((from_inner, from_outer, lheld))
            inner[0], outer[0] = from_inner, from_outer
            lprev = passed_along(later)
        earlier = own[:-1] if step == ITERS - 1 else []
        nxt, rounded, long, *sums = apply_ham(
            own[-1], from_inner, from_outer, lheld, rheld, mpo, charge, limit, odd, earlier, peers
        )
        own.append(nxt)
    from_inner, from_outer = neighbours(rounded, long)
    inner.append(from_inner)
    outer.append(from_outer)
    sums = lax.all_to_all(sums[0], "blk", 0, 0)
    ext, energy = combine(own, inner, outer, sums, mpo, charge, odd, chans, width)
    arrived = passed_along(ext)
    first = (lax.axis_index("seg") == 0).astype(jnp.int32).reshape(1)
    merged = env_of(arrived, lprev, lheld, mpo, charge, first, factor)
    return ext[1][None, None], energy[0, :1], merged[None, :, None]


def solution(mesh):
    placed = (
        P("seg", "blk", None, None),
        P("seg", None, "blk", None, None),
        P("seg", None, "blk", None, None),
        P(),
        P(),
        P("seg", "blk"),
    )
    return jax.shard_map(
        on_device,
        mesh=mesh,
        in_specs=placed,
        out_specs=(P("seg", "blk", None, None), P("seg"), P("seg", None, "blk", None, None)),
        check_vma=False,
    )
```

```python
import functools

import jax
import jax.numpy as jnp
from jax import lax
from jax.experimental import pallas as pl
from jax.experimental.pallas import tpu as pltpu
from jax.sharding import PartitionSpec as P

ITERS = 3
SHRINK = 2.0**-12
VMEM_LIMIT = 48 << 20
EXTRA = ((0, 16), (0, 16), (0, 16), (0, 16))
PIECES = ((0, 22), (12, 30))
GROUP = 4

SMEM_SPEC = pl.BlockSpec(memory_space=pltpu.SMEM)
VMEM_SPEC = pl.BlockSpec(memory_space=pltpu.VMEM)


def kernel_call(body, out_shape, out_specs, in_specs, name, scratch=()):
    return pl.pallas_call(
        body,
        out_shape=out_shape,
        in_specs=in_specs,
        out_specs=out_specs,
        scratch_shapes=scratch,
        name=name,
        compiler_params=pltpu.CompilerParams(vmem_limit_bytes=VMEM_LIMIT),
    )


def shift_of(mpo_ref, charge_ref, chans, phys):
    total = jnp.float32(0.0)
    for a in range(chans):
        trace = mpo_ref[a * phys * phys]
        for i in range(1, phys):
            trace = trace + mpo_ref[a * phys * phys + i * (phys + 1)]
        total = total + jnp.where(charge_ref[a] == 0, trace, 0.0)
    return 2.0 + total * (1.0 / phys)


def mixed_blocks(a, ext_ref, l_ref, mpo_ref, charge_ref, width, phys):
    product = jnp.dot(l_ref[a], ext_ref[1 - charge_ref[a]], preferred_element_type=jnp.float32)
    blocks = []
    for i in range(phys):
        total = None
        for q in range(phys):
            term = mpo_ref[a * phys * phys + i * phys + q] * product[:, q * width : (q + 1) * width]
            total = term if total is None else total + term
        blocks.append(total.astype(jnp.bfloat16))
    return jnp.concatenate(blocks, axis=0)


def mixed_group(chosen, *rest):
    return jnp.concatenate([mixed_blocks(a, *rest) for a in chosen], axis=1)


def set_neighbours(ext_ref, odd, inner, outer):
    rows = ext_ref.shape[1]
    ext_ref[2 - 2 * odd] = inner[:rows]
    ext_ref[2 * odd] = outer[:rows]


def total_of(values):
    return jnp.sum(jnp.sum(values, axis=0, keepdims=True), axis=1, keepdims=True)


def pairs_of(count):
    return [(a, b) for a in range(count) for b in range(a, count)]


def apply_kernel(chans, width, phys, history, mpo_ref, charge_ref, kept_ref, odd_ref, own_ref, inner_ref, outer_ref, l_ref, r_ref, *refs):
    earlier = refs[:history]
    outs = refs[history:-1]
    ext_ref = refs[-1]
    own = own_ref[:width].astype(jnp.float32)
    ext_ref[1] = own.astype(jnp.bfloat16)
    set_neighbours(ext_ref, odd_ref[0], inner_ref[...], outer_ref[...])
    total = None
    for first in range(0, chans, GROUP):
        chosen = range(first, min(first + GROUP, chans))
        lhs = mixed_group(chosen, ext_ref, l_ref, mpo_ref, charge_ref, width, phys)
        rhs = r_ref[first : first + len(chosen)].reshape(len(chosen) * width, width)
        term = jnp.dot(lhs, rhs, preferred_element_type=jnp.float32)
        total = term if total is None else total + term
    kept = kept_ref[0]
    rows = lax.broadcasted_iota(jnp.int32, (width, width), 0)
    cols = lax.broadcasted_iota(jnp.int32, (width, width), 1)
    mask = (rows < kept) & (cols < kept)
    shift = shift_of(mpo_ref, charge_ref, chans, phys)
    parts = []
    for i in range(phys):
        cut = slice(i * width, (i + 1) * width)
        part = SHRINK * (jnp.where(mask, total[cut, :], 0.0) - shift * own[:, cut])
        outs[0][:, cut] = part
        parts.append(part)
    fill_sent(outs[1:3], jnp.concatenate(parts, axis=1).astype(jnp.bfloat16))
    if history:
        vectors = [ref[:width].astype(jnp.float32) for ref in earlier] + [own, jnp.concatenate(parts, axis=1)]
        lane = lax.broadcasted_iota(jnp.int32, (1, width), 1)
        row = jnp.zeros((1, width), jnp.float32)
        for k, (a, b) in enumerate(pairs_of(len(vectors))):
            row = row + jnp.where(lane == k, total_of(vectors[a] * vectors[b]), 0.0)
        outs[3][...] = jnp.broadcast_to(row[None], outs[3].shape)


def sent_shapes(shape, step):
    rows, cols = shape
    return [jax.ShapeDtypeStruct((rows + more, cols), jnp.bfloat16) for more in EXTRA[step]]


def fill_sent(refs, x):
    rows = x.shape[0]
    for ref in refs:
        ref[:rows] = x
        if ref.shape[0] > rows:
            ref[rows:] = jnp.zeros((ref.shape[0] - rows, x.shape[1]), x.dtype)


def apply_ham(own, inner, outer, lenv, renv, mpo, charge, kept, odd, earlier, peers, step):
    chans, width, _ = lenv.shape
    phys = own.shape[1] // width
    shape = (width, own.shape[1])
    shapes = [jax.ShapeDtypeStruct(shape, jnp.float32), *sent_shapes(shape, step)]
    if earlier:
        shapes.append(jax.ShapeDtypeStruct((peers, 1, width), jnp.float32))
    return kernel_call(
        functools.partial(apply_kernel, chans, width, phys, len(earlier)),
        shapes,
        [VMEM_SPEC] * len(shapes),
        [SMEM_SPEC] * 4 + [VMEM_SPEC] * (5 + len(earlier)),
        "apply_ham",
        [pltpu.VMEM((3, *shape), jnp.bfloat16)],
    )(mpo, charge, kept, odd, own, inner, outer, lenv, renv, *earlier)


def combine_kernel(chans, phys, mpo_ref, charge_ref, odd_ref, sums_ref, *refs):
    count = ITERS + 1
    own, inner_refs, outer_refs = refs[:count], refs[count : 2 * count], refs[2 * count : 3 * count]
    ext_ref, energy_ref = refs[3 * count :]
    shift = shift_of(mpo_ref, charge_ref, chans, phys)
    row = jnp.sum(sums_ref[...], axis=0)
    lane = lax.broadcasted_iota(jnp.int32, row.shape, 1)
    gram = {}
    for k, (a, b) in enumerate(pairs_of(count)):
        gram[a, b] = gram[b, a] = jnp.sum(jnp.where(lane == k, row, 0.0), axis=1, keepdims=True)

    def product(p, q):
        total = None
        for a, pa in enumerate(p):
            for b, qb in enumerate(q):
                term = gram[a, b] * (pa * qb)
                total = term if total is None else total + term
        return total

    p = [jnp.ones((1, 1), jnp.float32)]
    energy = None
    for _ in range(ITERS):
        hp = [shift * c for c in p] + [jnp.zeros((1, 1), jnp.float32)]
        for k, c in enumerate(p):
            hp[k + 1] = hp[k + 1] + (1.0 / SHRINK) * c
        rr, xh, hh = product(p, p), product(p, hp), product(hp, hp)
        energy = xh / rr
        rres = jnp.maximum(hh - energy * xh, 0.0)
        scale = 1.0 / jnp.sqrt(rr + 0.25 * rres)
        grown = p + [jnp.zeros((1, 1), jnp.float32)]
        p = [scale * (c - 0.5 * (h - energy * c)) for c, h in zip(grown, hp)]
    def final(vectors):
        x = None
        for c, ref in zip(p, vectors):
            term = c * ref[: ext_ref.shape[1]].astype(jnp.float32)
            x = term if x is None else x + term
        return x.astype(jnp.bfloat16)

    ext_ref[1] = final(own)
    set_neighbours(ext_ref, odd_ref[0], final(inner_refs), final(outer_refs))
    energy_ref[...] = jnp.broadcast_to(energy, energy_ref.shape)


def combine(own, inner, outer, sums, mpo, charge, odd, chans, width):
    phys = own[0].shape[1] // width
    return kernel_call(
        functools.partial(combine_kernel, chans, phys),
        [jax.ShapeDtypeStruct((3, width, own[0].shape[1]), jnp.bfloat16), jax.ShapeDtypeStruct((8, width), jnp.float32)],
        [VMEM_SPEC] * 2,
        [SMEM_SPEC] * 3 + [VMEM_SPEC] * (1 + 3 * len(own)),
        "combine",
    )(mpo, charge, odd, sums, *own, *inner, *outer)


def env_kernel(chans, width, phys, factor, mpo_ref, charge_ref, first_ref, ext_ref, own_l_ref, *refs):
    *l_refs, out_ref, cols_ref, turned_ref, made_ref, sems = refs
    found = {a: (ref, a - low) for ref, (low, high) in zip(l_refs, PIECES) for a in range(low, high)}
    parts = [pl.ds(2 * pair, 2) for pair in range(chans // 2)]

    @pl.when(first_ref[0] != 0)
    def _():
        for k, (source, target) in enumerate(((own_l_ref, made_ref), (made_ref, out_ref))):
            copy = pltpu.make_async_copy(source, target, sems.at[k])
            copy.start()
            copy.wait()

    @pl.when(first_ref[0] == 0)
    def _():
        for i in range(phys):
            cut = slice(i * width, (i + 1) * width)
            for place in range(3):
                cols_ref[place, cut, :] = ext_ref[place, :, cut]
            turned_ref[cut, :] = ext_ref[1, :, cut].astype(jnp.float32).T.astype(jnp.bfloat16)
        copies = []
        for pair, part in enumerate(parts):
            sources = [found[a] for a in (2 * pair, 2 * pair + 1)]
            both = jnp.concatenate([ref[k] for ref, k in sources], axis=1)
            left = jnp.dot(turned_ref[...], both, preferred_element_type=jnp.float32)
            for k in range(2):
                a = 2 * pair + k
                blocks = []
                for q in range(phys):
                    total = None
                    for i in range(phys):
                        cut = left[i * width : (i + 1) * width, k * width : (k + 1) * width]
                        term = mpo_ref[a * phys * phys + i * phys + q] * cut
                        total = term if total is None else total + term
                    blocks.append(total.astype(jnp.bfloat16))
                made = jnp.dot(
                    jnp.concatenate(blocks, axis=1), cols_ref[1 - charge_ref[a]], preferred_element_type=jnp.float32
                )
                made_ref[a] = (factor * made).astype(jnp.bfloat16)
            copies.append(pltpu.make_async_copy(made_ref.at[part], out_ref.at[part], sems.at[pair]))
            copies[-1].start()
        for copy in copies:
            copy.wait()


def env_of(ext, lprev, lenv, mpo, charge, first, factor):
    chans, width, _ = lenv.shape
    phys = ext.shape[2] // width
    return kernel_call(
        functools.partial(env_kernel, chans, width, phys, factor),
        jax.ShapeDtypeStruct(lenv.shape, jnp.bfloat16),
        pl.BlockSpec(memory_space=pl.ANY),
        [SMEM_SPEC] * 3 + [VMEM_SPEC, pl.BlockSpec(memory_space=pl.ANY)] + [VMEM_SPEC] * len(lprev),
        "new_env",
        [
            pltpu.VMEM((3, phys * width, width), jnp.bfloat16),
            pltpu.VMEM((phys * width, width), jnp.bfloat16),
            pltpu.VMEM(lenv.shape, jnp.bfloat16),
            pltpu.SemaphoreType.DMA((chans // 2,)),
        ],
    )(mpo, charge, first, ext, lenv, *lprev)


def hold_kernel(*refs):
    pass


def held_in_vmem(lenv, renv, charge, mpo):
    return pl.pallas_call(
        hold_kernel,
        out_shape=[jax.ShapeDtypeStruct(array.shape, array.dtype) for array in (lenv, renv)],
        in_specs=[VMEM_SPEC] * 2 + [SMEM_SPEC] * 2,
        out_specs=[VMEM_SPEC] * 2,
        input_output_aliases={0: 0, 1: 1},
        name="hold",
        compiler_params=pltpu.CompilerParams(vmem_limit_bytes=VMEM_LIMIT),
    )(lenv, renv, charge, mpo)


def mask_kernel(width, kept_ref, site_ref, out_ref, long_ref):
    kept = kept_ref[0]
    rows = lax.broadcasted_iota(jnp.int32, site_ref.shape, 0)
    cols = lax.broadcasted_iota(jnp.int32, site_ref.shape, 1) % width
    site = site_ref[...].astype(jnp.float32)
    site = jnp.where((rows < kept) & (cols < kept), site, 0.0).astype(jnp.bfloat16)
    fill_sent((out_ref, long_ref), site)


def masked(site, kept):
    width = site.shape[0]
    return kernel_call(
        functools.partial(mask_kernel, width),
        sent_shapes(site.shape, 0),
        [VMEM_SPEC] * 2,
        [SMEM_SPEC, VMEM_SPEC],
        "masked",
    )(kept, site)


def neighbours(x, long):
    count = lax.axis_size("blk")
    outer = lax.ppermute(long, "blk", [(i, i + 1 if i % 2 else i - 1) for i in range(1, count - 1)])
    inner = lax.ppermute(x, "blk", [(i, i ^ 1) for i in range(count)])
    return inner, outer


def passed_along(array):
    length = lax.axis_size("seg")
    return lax.ppermute(array, "seg", [(i, i + 1) for i in range(length - 1)])


def on_device(site, left_env, right_env, mpo, charge, kept):
    width = site.shape[2]
    chans = left_env.shape[1]
    peers = lax.axis_size("blk")
    factor = float(site.shape[1] * peers * width * width)
    lenv = left_env[0, :, 0]
    renv = right_env[0, :, 0]
    mpo = mpo.reshape(-1)
    limit = kept[0]
    x, long = masked(site[0, 0], limit)
    lheld, rheld = held_in_vmem(lenv, renv, charge, mpo)
    odd = (lax.axis_index("blk") % 2).astype(jnp.int32).reshape(1)
    own, inner, outer = [x], [], []
    rounded = x
    for step in range(ITERS):
        from_inner, from_outer = neighbours(rounded, long)
        inner.append(from_inner)
        outer.append(from_outer)
        if step == 0:
            from_inner, from_outer, later = lax.optimization_barrier((from_inner, from_outer, lheld))
            inner[0], outer[0] = from_inner, from_outer
            lprev = [passed_along(later[a:b]) for a, b in PIECES]
        earlier = own[:-1] if step == ITERS - 1 else []
        nxt, rounded, long, *sums = apply_ham(
            own[-1], from_inner, from_outer, lheld, rheld, mpo, charge, limit, odd, earlier, peers, step + 1
        )
        own.append(nxt)
    from_inner, from_outer = neighbours(rounded, long)
    inner.append(from_inner)
    outer.append(from_outer)
    sums = lax.all_to_all(sums[0], "blk", 0, 0)
    ext, energy = combine(own, inner, outer, sums, mpo, charge, odd, chans, width)
    arrived = passed_along(ext)
    first = (lax.axis_index("seg") == 0).astype(jnp.int32).reshape(1)
    merged = env_of(arrived, lprev, lenv, mpo, charge, first, factor)
    return ext[1][None, None], energy[0, :1], merged[None, :, None]


def solution(mesh):
    placed = (
        P("seg", "blk", None, None),
        P("seg", None, "blk", None, None),
        P("seg", None, "blk", None, None),
        P(),
        P(),
        P("seg", "blk"),
    )
    return jax.shard_map(
        on_device,
        mesh=mesh,
        in_specs=placed,
        out_specs=(P("seg", "blk", None, None), P("seg"), P("seg", None, "blk", None, None)),
        check_vma=False,
    )
```

```python
import functools

import jax
import jax.numpy as jnp
from jax import lax
from jax.experimental import pallas as pl
from jax.experimental.pallas import tpu as pltpu
from jax.sharding import PartitionSpec as P

ITERS = 3
SHRINK = 2.0**-12
VMEM_LIMIT = 48 << 20
EXTRA = ((0, 16), (0, 16), (0, 16), (0, 16))
PIECES = ((0, 22), (12, 30))
GROUP = 4

SMEM_SPEC = pl.BlockSpec(memory_space=pltpu.SMEM)
VMEM_SPEC = pl.BlockSpec(memory_space=pltpu.VMEM)


def kernel_call(body, out_shape, out_specs, in_specs, name, scratch=()):
    return pl.pallas_call(
        body,
        out_shape=out_shape,
        in_specs=in_specs,
        out_specs=out_specs,
        scratch_shapes=scratch,
        name=name,
        compiler_params=pltpu.CompilerParams(vmem_limit_bytes=VMEM_LIMIT),
    )


def shift_of(mpo_ref, charge_ref, chans, phys):
    total = jnp.float32(0.0)
    for a in range(chans):
        trace = mpo_ref[a * phys * phys]
        for i in range(1, phys):
            trace = trace + mpo_ref[a * phys * phys + i * (phys + 1)]
        total = total + jnp.where(charge_ref[a] == 0, trace, 0.0)
    return 2.0 + total * (1.0 / phys)


def mixed_blocks(a, ext_ref, l_ref, mpo_ref, charge_ref, width, phys):
    product = jnp.dot(l_ref[a], ext_ref[1 - charge_ref[a]], preferred_element_type=jnp.float32)
    blocks = []
    for i in range(phys):
        total = None
        for q in range(phys):
            term = mpo_ref[a * phys * phys + i * phys + q] * product[:, q * width : (q + 1) * width]
            total = term if total is None else total + term
        blocks.append(total.astype(jnp.bfloat16))
    return jnp.concatenate(blocks, axis=0)


def mixed_group(chosen, *rest):
    return jnp.concatenate([mixed_blocks(a, *rest) for a in chosen], axis=1)


def set_neighbours(ext_ref, odd, inner, outer):
    rows = ext_ref.shape[1]
    ext_ref[2 - 2 * odd] = inner[:rows]
    ext_ref[2 * odd] = outer[:rows]


def total_of(values):
    return jnp.sum(jnp.sum(values, axis=0, keepdims=True), axis=1, keepdims=True)


def pairs_of(count):
    return [(a, b) for a in range(count) for b in range(a, count)]


def apply_kernel(chans, width, phys, history, mpo_ref, charge_ref, kept_ref, odd_ref, own_ref, inner_ref, outer_ref, l_ref, r_ref, *refs):
    earlier = refs[:history]
    outs = refs[history:-1]
    ext_ref = refs[-1]
    own = own_ref[:width].astype(jnp.float32)
    ext_ref[1] = own.astype(jnp.bfloat16)
    set_neighbours(ext_ref, odd_ref[0], inner_ref[...], outer_ref[...])
    total = None
    for first in range(0, chans, GROUP):
        chosen = range(first, min(first + GROUP, chans))
        lhs = mixed_group(chosen, ext_ref, l_ref, mpo_ref, charge_ref, width, phys)
        rhs = r_ref[first : first + len(chosen)].reshape(len(chosen) * width, width)
        term = jnp.dot(lhs, rhs, preferred_element_type=jnp.float32)
        total = term if total is None else total + term
    kept = kept_ref[0]
    rows = lax.broadcasted_iota(jnp.int32, (width, width), 0)
    cols = lax.broadcasted_iota(jnp.int32, (width, width), 1)
    mask = (rows < kept) & (cols < kept)
    shift = shift_of(mpo_ref, charge_ref, chans, phys)
    parts = []
    for i in range(phys):
        cut = slice(i * width, (i + 1) * width)
        part = SHRINK * (jnp.where(mask, total[cut, :], 0.0) - shift * own[:, cut])
        outs[0][:, cut] = part
        parts.append(part)
    fill_sent(outs[1:3], jnp.concatenate(parts, axis=1).astype(jnp.bfloat16))
    if history:
        vectors = [ref[:width].astype(jnp.float32) for ref in earlier] + [own, jnp.concatenate(parts, axis=1)]
        lane = lax.broadcasted_iota(jnp.int32, (1, width), 1)
        row = jnp.zeros((1, width), jnp.float32)
        for k, (a, b) in enumerate(pairs_of(len(vectors))):
            row = row + jnp.where(lane == k, total_of(vectors[a] * vectors[b]), 0.0)
        outs[3][...] = jnp.broadcast_to(row[None], outs[3].shape)


def sent_shapes(shape, step):
    rows, cols = shape
    return [jax.ShapeDtypeStruct((rows + more, cols), jnp.bfloat16) for more in EXTRA[step]]


def fill_sent(refs, x):
    rows = x.shape[0]
    for ref in refs:
        ref[:rows] = x
        if ref.shape[0] > rows:
            ref[rows:] = jnp.zeros((ref.shape[0] - rows, x.shape[1]), x.dtype)


def apply_ham(own, inner, outer, lenv, renv, mpo, charge, kept, odd, earlier, peers, step):
    chans, width, _ = lenv.shape
    phys = own.shape[1] // width
    shape = (width, own.shape[1])
    shapes = [jax.ShapeDtypeStruct(shape, jnp.float32), *sent_shapes(shape, step)]
    if earlier:
        shapes.append(jax.ShapeDtypeStruct((peers, 1, width), jnp.float32))
    return kernel_call(
        functools.partial(apply_kernel, chans, width, phys, len(earlier)),
        shapes,
        [VMEM_SPEC] * len(shapes),
        [SMEM_SPEC] * 4 + [VMEM_SPEC] * (5 + len(earlier)),
        "apply_ham",
        [pltpu.VMEM((3, *shape), jnp.bfloat16)],
    )(mpo, charge, kept, odd, own, inner, outer, lenv, renv, *earlier)


def combine_kernel(chans, phys, mpo_ref, charge_ref, odd_ref, sums_ref, *refs):
    count = ITERS + 1
    own, inner_refs, outer_refs = refs[:count], refs[count : 2 * count], refs[2 * count : 3 * count]
    ext_ref, energy_ref = refs[3 * count :]
    shift = shift_of(mpo_ref, charge_ref, chans, phys)
    row = jnp.sum(sums_ref[...], axis=0)
    lane = lax.broadcasted_iota(jnp.int32, row.shape, 1)
    gram = {}
    for k, (a, b) in enumerate(pairs_of(count)):
        gram[a, b] = gram[b, a] = jnp.sum(jnp.where(lane == k, row, 0.0), axis=1, keepdims=True)

    def product(p, q):
        total = None
        for a, pa in enumerate(p):
            for b, qb in enumerate(q):
                term = gram[a, b] * (pa * qb)
                total = term if total is None else total + term
        return total

    p = [jnp.ones((1, 1), jnp.float32)]
    energy = None
    for _ in range(ITERS):
        hp = [shift * c for c in p] + [jnp.zeros((1, 1), jnp.float32)]
        for k, c in enumerate(p):
            hp[k + 1] = hp[k + 1] + (1.0 / SHRINK) * c
        rr, xh, hh = product(p, p), product(p, hp), product(hp, hp)
        energy = xh / rr
        rres = jnp.maximum(hh - energy * xh, 0.0)
        scale = 1.0 / jnp.sqrt(rr + 0.25 * rres)
        grown = p + [jnp.zeros((1, 1), jnp.float32)]
        p = [scale * (c - 0.5 * (h - energy * c)) for c, h in zip(grown, hp)]
    def final(vectors):
        x = None
        for c, ref in zip(p, vectors):
            term = c * ref[: ext_ref.shape[1]].astype(jnp.float32)
            x = term if x is None else x + term
        return x.astype(jnp.bfloat16)

    ext_ref[1] = final(own)
    set_neighbours(ext_ref, odd_ref[0], final(inner_refs), final(outer_refs))
    energy_ref[...] = jnp.broadcast_to(energy, energy_ref.shape)


def combine(own, inner, outer, sums, mpo, charge, odd, chans, width):
    phys = own[0].shape[1] // width
    return kernel_call(
        functools.partial(combine_kernel, chans, phys),
        [jax.ShapeDtypeStruct((3, width, own[0].shape[1]), jnp.bfloat16), jax.ShapeDtypeStruct((8, width), jnp.float32)],
        [VMEM_SPEC] * 2,
        [SMEM_SPEC] * 3 + [VMEM_SPEC] * (1 + 3 * len(own)),
        "combine",
    )(mpo, charge, odd, sums, *own, *inner, *outer)


def env_kernel(chans, width, phys, factor, mpo_ref, charge_ref, first_ref, ext_ref, own_l_ref, l_ref, out_ref, cols_ref, turned_ref, made_ref, sems):
    parts = [pl.ds(2 * pair, 2) for pair in range(chans // 2)]

    @pl.when(first_ref[0] != 0)
    def _():
        for k, (source, target) in enumerate(((own_l_ref, made_ref), (made_ref, out_ref))):
            copy = pltpu.make_async_copy(source, target, sems.at[k])
            copy.start()
            copy.wait()

    @pl.when(first_ref[0] == 0)
    def _():
        for i in range(phys):
            cut = slice(i * width, (i + 1) * width)
            for place in range(3):
                cols_ref[place, cut, :] = ext_ref[place, :, cut]
            turned_ref[cut, :] = ext_ref[1, :, cut].astype(jnp.float32).T.astype(jnp.bfloat16)
        copies = []
        for pair, part in enumerate(parts):
            both = jnp.concatenate([l_ref[2 * pair], l_ref[2 * pair + 1]], axis=1)
            left = jnp.dot(turned_ref[...], both, preferred_element_type=jnp.float32)
            for k in range(2):
                a = 2 * pair + k
                blocks = []
                for q in range(phys):
                    total = None
                    for i in range(phys):
                        cut = left[i * width : (i + 1) * width, k * width : (k + 1) * width]
                        term = mpo_ref[a * phys * phys + i * phys + q] * cut
                        total = term if total is None else total + term
                    blocks.append(total.astype(jnp.bfloat16))
                made = jnp.dot(
                    jnp.concatenate(blocks, axis=1), cols_ref[1 - charge_ref[a]], preferred_element_type=jnp.float32
                )
                made_ref[a] = (factor * made).astype(jnp.bfloat16)
            copies.append(pltpu.make_async_copy(made_ref.at[part], out_ref.at[part], sems.at[pair]))
            copies[-1].start()
        for copy in copies:
            copy.wait()


def env_of(ext, lprev, lenv, mpo, charge, first, factor):
    chans, width, _ = lenv.shape
    phys = ext.shape[2] // width
    return kernel_call(
        functools.partial(env_kernel, chans, width, phys, factor),
        jax.ShapeDtypeStruct(lenv.shape, jnp.bfloat16),
        pl.BlockSpec(memory_space=pl.ANY),
        [SMEM_SPEC] * 3 + [VMEM_SPEC, pl.BlockSpec(memory_space=pl.ANY), VMEM_SPEC],
        "new_env",
        [
            pltpu.VMEM((3, phys * width, width), jnp.bfloat16),
            pltpu.VMEM((phys * width, width), jnp.bfloat16),
            pltpu.VMEM(lenv.shape, jnp.bfloat16),
            pltpu.SemaphoreType.DMA((chans // 2,)),
        ],
    )(mpo, charge, first, ext, lenv, lprev)


def join_kernel(*refs):
    *pieces, out_ref, sems = refs
    copies = []
    ends = [low for low, _ in PIECES[1:]] + [PIECES[-1][1]]
    for k, (piece, (low, _), end) in enumerate(zip(pieces, PIECES, ends)):
        copies.append(
            pltpu.make_async_copy(piece.at[pl.ds(0, end - low)], out_ref.at[pl.ds(low, end - low)], sems.at[k])
        )
        copies[-1].start()
    for copy in copies:
        copy.wait()


def joined(pieces):
    _, width, _ = pieces[0].shape
    return kernel_call(
        join_kernel,
        jax.ShapeDtypeStruct((PIECES[-1][1], width, width), pieces[0].dtype),
        VMEM_SPEC,
        [pl.BlockSpec(memory_space=pl.ANY)] * len(pieces),
        "join",
        [pltpu.SemaphoreType.DMA((len(pieces),))],
    )(*pieces)


def hold_kernel(*refs):
    pass


def held_in_vmem(lenv, renv, charge, mpo):
    return pl.pallas_call(
        hold_kernel,
        out_shape=[jax.ShapeDtypeStruct(array.shape, array.dtype) for array in (lenv, renv)],
        in_specs=[VMEM_SPEC] * 2 + [SMEM_SPEC] * 2 + [pl.BlockSpec(memory_space=pl.ANY)],
        out_specs=[VMEM_SPEC] * 2,
        input_output_aliases={0: 0, 1: 1},
        name="hold",
        compiler_params=pltpu.CompilerParams(vmem_limit_bytes=VMEM_LIMIT),
    )(lenv, renv, charge, mpo, renv)


def mask_kernel(width, kept_ref, site_ref, out_ref, long_ref):
    kept = kept_ref[0]
    rows = lax.broadcasted_iota(jnp.int32, site_ref.shape, 0)
    cols = lax.broadcasted_iota(jnp.int32, site_ref.shape, 1) % width
    site = site_ref[...].astype(jnp.float32)
    site = jnp.where((rows < kept) & (cols < kept), site, 0.0).astype(jnp.bfloat16)
    fill_sent((out_ref, long_ref), site)


def masked(site, kept):
    width = site.shape[0]
    return kernel_call(
        functools.partial(mask_kernel, width),
        sent_shapes(site.shape, 0),
        [VMEM_SPEC] * 2,
        [SMEM_SPEC, VMEM_SPEC],
        "masked",
    )(kept, site)


def neighbours(x, long):
    count = lax.axis_size("blk")
    outer = lax.ppermute(long, "blk", [(i, i + 1 if i % 2 else i - 1) for i in range(1, count - 1)])
    inner = lax.ppermute(x, "blk", [(i, i ^ 1) for i in range(count)])
    return inner, outer


def passed_along(array):
    length = lax.axis_size("seg")
    return lax.ppermute(array, "seg", [(i, i + 1) for i in range(length - 1)])


def on_device(site, left_env, right_env, mpo, charge, kept):
    width = site.shape[2]
    chans = left_env.shape[1]
    peers = lax.axis_size("blk")
    factor = float(site.shape[1] * peers * width * width)
    lenv = left_env[0, :, 0]
    renv = right_env[0, :, 0]
    mpo = mpo.reshape(-1)
    limit = kept[0]
    x, long = masked(site[0, 0], limit)
    lheld, rheld = held_in_vmem(lenv, renv, charge, mpo)
    odd = (lax.axis_index("blk") % 2).astype(jnp.int32).reshape(1)
    own, inner, outer = [x], [], []
    rounded = x
    for step in range(ITERS):
        from_inner, from_outer = neighbours(rounded, long)
        inner.append(from_inner)
        outer.append(from_outer)
        if step == 0:
            from_inner, from_outer, later = lax.optimization_barrier((from_inner, from_outer, lheld))
            inner[0], outer[0] = from_inner, from_outer
            lprev = [passed_along(later[a:b]) for a, b in PIECES]
        earlier = own[:-1] if step == ITERS - 1 else []
        nxt, rounded, long, *sums = apply_ham(
            own[-1], from_inner, from_outer, lheld, rheld, mpo, charge, limit, odd, earlier, peers, step + 1
        )
        own.append(nxt)
    from_inner, from_outer = neighbours(rounded, long)
    inner.append(from_inner)
    outer.append(from_outer)
    sums = lax.all_to_all(sums[0], "blk", 0, 0)
    ext, energy = combine(own, inner, outer, sums, mpo, charge, odd, chans, width)
    arrived = passed_along(ext)
    first = (lax.axis_index("seg") == 0).astype(jnp.int32).reshape(1)
    merged = env_of(arrived, joined(lprev), lenv, mpo, charge, first, factor)
    return ext[1][None, None], energy[0, :1], merged[None, :, None]


def solution(mesh):
    placed = (
        P("seg", "blk", None, None),
        P("seg", None, "blk", None, None),
        P("seg", None, "blk", None, None),
        P(),
        P(),
        P("seg", "blk"),
    )
    return jax.shard_map(
        on_device,
        mesh=mesh,
        in_specs=placed,
        out_specs=(P("seg", "blk", None, None), P("seg"), P("seg", None, "blk", None, None)),
        check_vma=False,
    )
```

```python
import functools

import jax
import jax.numpy as jnp
from jax import lax
from jax.experimental import pallas as pl
from jax.experimental.pallas import tpu as pltpu
from jax.sharding import PartitionSpec as P

ITERS = 3
SHRINK = 2.0**-12
VMEM_LIMIT = 48 << 20
EXTRA = ((0, 16), (0, 16), (0, 16), (16, 0))
PIECES = ((0, 22), (12, 30))
GROUP = 4

SMEM_SPEC = pl.BlockSpec(memory_space=pltpu.SMEM)
VMEM_SPEC = pl.BlockSpec(memory_space=pltpu.VMEM)


def kernel_call(body, out_shape, out_specs, in_specs, name, scratch=()):
    return pl.pallas_call(
        body,
        out_shape=out_shape,
        in_specs=in_specs,
        out_specs=out_specs,
        scratch_shapes=scratch,
        name=name,
        compiler_params=pltpu.CompilerParams(vmem_limit_bytes=VMEM_LIMIT),
    )


def shift_of(mpo_ref, charge_ref, chans, phys):
    total = jnp.float32(0.0)
    for a in range(chans):
        trace = mpo_ref[a * phys * phys]
        for i in range(1, phys):
            trace = trace + mpo_ref[a * phys * phys + i * (phys + 1)]
        total = total + jnp.where(charge_ref[a] == 0, trace, 0.0)
    return 2.0 + total * (1.0 / phys)


def mixed_blocks(a, ext_ref, l_ref, mpo_ref, charge_ref, width, phys):
    product = jnp.dot(l_ref[a], ext_ref[1 - charge_ref[a]], preferred_element_type=jnp.float32)
    blocks = []
    for i in range(phys):
        total = None
        for q in range(phys):
            term = mpo_ref[a * phys * phys + i * phys + q] * product[:, q * width : (q + 1) * width]
            total = term if total is None else total + term
        blocks.append(total.astype(jnp.bfloat16))
    return jnp.concatenate(blocks, axis=0)


def mixed_group(chosen, *rest):
    return jnp.concatenate([mixed_blocks(a, *rest) for a in chosen], axis=1)


def set_neighbours(ext_ref, odd, inner, outer):
    rows = ext_ref.shape[1]
    ext_ref[2 - 2 * odd] = inner[:rows]
    ext_ref[2 * odd] = outer[:rows]


def total_of(values):
    return jnp.sum(jnp.sum(values, axis=0, keepdims=True), axis=1, keepdims=True)


def pairs_of(count):
    return [(a, b) for a in range(count) for b in range(a, count)]


def apply_kernel(chans, width, phys, history, mpo_ref, charge_ref, kept_ref, odd_ref, own_ref, inner_ref, outer_ref, l_ref, r_ref, *refs):
    earlier = refs[:history]
    outs = refs[history:-1]
    ext_ref = refs[-1]
    own = own_ref[:width].astype(jnp.float32)
    ext_ref[1] = own.astype(jnp.bfloat16)
    set_neighbours(ext_ref, odd_ref[0], inner_ref[...], outer_ref[...])
    total = None
    for first in range(0, chans, GROUP):
        chosen = range(first, min(first + GROUP, chans))
        lhs = mixed_group(chosen, ext_ref, l_ref, mpo_ref, charge_ref, width, phys)
        rhs = r_ref[first : first + len(chosen)].reshape(len(chosen) * width, width)
        term = jnp.dot(lhs, rhs, preferred_element_type=jnp.float32)
        total = term if total is None else total + term
    kept = kept_ref[0]
    rows = lax.broadcasted_iota(jnp.int32, (width, width), 0)
    cols = lax.broadcasted_iota(jnp.int32, (width, width), 1)
    mask = (rows < kept) & (cols < kept)
    shift = shift_of(mpo_ref, charge_ref, chans, phys)
    parts = []
    for i in range(phys):
        cut = slice(i * width, (i + 1) * width)
        part = SHRINK * (jnp.where(mask, total[cut, :], 0.0) - shift * own[:, cut])
        outs[0][:, cut] = part
        parts.append(part)
    fill_sent(outs[1:3], jnp.concatenate(parts, axis=1).astype(jnp.bfloat16))
    if history:
        vectors = [ref[:width].astype(jnp.float32) for ref in earlier] + [own, jnp.concatenate(parts, axis=1)]
        lane = lax.broadcasted_iota(jnp.int32, (1, width), 1)
        row = jnp.zeros((1, width), jnp.float32)
        for k, (a, b) in enumerate(pairs_of(len(vectors))):
            row = row + jnp.where(lane == k, total_of(vectors[a] * vectors[b]), 0.0)
        outs[3][...] = jnp.broadcast_to(row[None], outs[3].shape)


def sent_shapes(shape, step):
    rows, cols = shape
    return [jax.ShapeDtypeStruct((rows + more, cols), jnp.bfloat16) for more in EXTRA[step]]


def fill_sent(refs, x):
    rows = x.shape[0]
    for ref in refs:
        ref[:rows] = x
        if ref.shape[0] > rows:
            ref[rows:] = jnp.zeros((ref.shape[0] - rows, x.shape[1]), x.dtype)


def apply_ham(own, inner, outer, lenv, renv, mpo, charge, kept, odd, earlier, peers, step):
    chans, width, _ = lenv.shape
    phys = own.shape[1] // width
    shape = (width, own.shape[1])
    shapes = [jax.ShapeDtypeStruct(shape, jnp.float32), *sent_shapes(shape, step)]
    if earlier:
        shapes.append(jax.ShapeDtypeStruct((peers, 1, width), jnp.float32))
    return kernel_call(
        functools.partial(apply_kernel, chans, width, phys, len(earlier)),
        shapes,
        [VMEM_SPEC] * len(shapes),
        [SMEM_SPEC] * 4 + [VMEM_SPEC] * (5 + len(earlier)),
        "apply_ham",
        [pltpu.VMEM((3, *shape), jnp.bfloat16)],
    )(mpo, charge, kept, odd, own, inner, outer, lenv, renv, *earlier)


def combine_kernel(chans, phys, mpo_ref, charge_ref, odd_ref, sums_ref, *refs):
    count = ITERS + 1
    own, inner_refs, outer_refs = refs[:count], refs[count : 2 * count], refs[2 * count : 3 * count]
    ext_ref, energy_ref = refs[3 * count :]
    shift = shift_of(mpo_ref, charge_ref, chans, phys)
    row = jnp.sum(sums_ref[...], axis=0)
    lane = lax.broadcasted_iota(jnp.int32, row.shape, 1)
    gram = {}
    for k, (a, b) in enumerate(pairs_of(count)):
        gram[a, b] = gram[b, a] = jnp.sum(jnp.where(lane == k, row, 0.0), axis=1, keepdims=True)

    def product(p, q):
        total = None
        for a, pa in enumerate(p):
            for b, qb in enumerate(q):
                term = gram[a, b] * (pa * qb)
                total = term if total is None else total + term
        return total

    p = [jnp.ones((1, 1), jnp.float32)]
    energy = None
    for _ in range(ITERS):
        hp = [shift * c for c in p] + [jnp.zeros((1, 1), jnp.float32)]
        for k, c in enumerate(p):
            hp[k + 1] = hp[k + 1] + (1.0 / SHRINK) * c
        rr, xh, hh = product(p, p), product(p, hp), product(hp, hp)
        energy = xh / rr
        rres = jnp.maximum(hh - energy * xh, 0.0)
        scale = 1.0 / jnp.sqrt(rr + 0.25 * rres)
        grown = p + [jnp.zeros((1, 1), jnp.float32)]
        p = [scale * (c - 0.5 * (h - energy * c)) for c, h in zip(grown, hp)]
    def final(vectors):
        x = None
        for c, ref in zip(p, vectors):
            term = c * ref[: ext_ref.shape[1]].astype(jnp.float32)
            x = term if x is None else x + term
        return x.astype(jnp.bfloat16)

    ext_ref[1] = final(own)
    set_neighbours(ext_ref, odd_ref[0], final(inner_refs), final(outer_refs))
    energy_ref[...] = jnp.broadcast_to(energy, energy_ref.shape)


def combine(own, inner, outer, sums, mpo, charge, odd, chans, width):
    phys = own[0].shape[1] // width
    return kernel_call(
        functools.partial(combine_kernel, chans, phys),
        [jax.ShapeDtypeStruct((3, width, own[0].shape[1]), jnp.bfloat16), jax.ShapeDtypeStruct((8, width), jnp.float32)],
        [VMEM_SPEC] * 2,
        [SMEM_SPEC] * 3 + [VMEM_SPEC] * (1 + 3 * len(own)),
        "combine",
    )(mpo, charge, odd, sums, *own, *inner, *outer)


def env_kernel(chans, width, phys, factor, mpo_ref, charge_ref, first_ref, ext_ref, own_l_ref, l_ref, out_ref, cols_ref, turned_ref, made_ref, sems):
    parts = [pl.ds(2 * pair, 2) for pair in range(chans // 2)]

    @pl.when(first_ref[0] != 0)
    def _():
        for k, (source, target) in enumerate(((own_l_ref, made_ref), (made_ref, out_ref))):
            copy = pltpu.make_async_copy(source, target, sems.at[k])
            copy.start()
            copy.wait()

    @pl.when(first_ref[0] == 0)
    def _():
        for i in range(phys):
            cut = slice(i * width, (i + 1) * width)
            for place in range(3):
                cols_ref[place, cut, :] = ext_ref[place, :, cut]
            turned_ref[cut, :] = ext_ref[1, :, cut].astype(jnp.float32).T.astype(jnp.bfloat16)
        copies = []
        for pair, part in enumerate(parts):
            both = jnp.concatenate([l_ref[2 * pair], l_ref[2 * pair + 1]], axis=1)
            left = jnp.dot(turned_ref[...], both, preferred_element_type=jnp.float32)
            for k in range(2):
                a = 2 * pair + k
                blocks = []
                for q in range(phys):
                    total = None
                    for i in range(phys):
                        cut = left[i * width : (i + 1) * width, k * width : (k + 1) * width]
                        term = mpo_ref[a * phys * phys + i * phys + q] * cut
                        total = term if total is None else total + term
                    blocks.append(total.astype(jnp.bfloat16))
                made = jnp.dot(
                    jnp.concatenate(blocks, axis=1), cols_ref[1 - charge_ref[a]], preferred_element_type=jnp.float32
                )
                made_ref[a] = (factor * made).astype(jnp.bfloat16)
            copies.append(pltpu.make_async_copy(made_ref.at[part], out_ref.at[part], sems.at[pair]))
            copies[-1].start()
        for copy in copies:
            copy.wait()


def env_of(ext, lprev, lenv, mpo, charge, first, factor):
    chans, width, _ = lenv.shape
    phys = ext.shape[2] // width
    return kernel_call(
        functools.partial(env_kernel, chans, width, phys, factor),
        jax.ShapeDtypeStruct(lenv.shape, jnp.bfloat16),
        pl.BlockSpec(memory_space=pl.ANY),
        [SMEM_SPEC] * 3 + [VMEM_SPEC, pl.BlockSpec(memory_space=pl.ANY), VMEM_SPEC],
        "new_env",
        [
            pltpu.VMEM((3, phys * width, width), jnp.bfloat16),
            pltpu.VMEM((phys * width, width), jnp.bfloat16),
            pltpu.VMEM(lenv.shape, jnp.bfloat16),
            pltpu.SemaphoreType.DMA((chans // 2,)),
        ],
    )(mpo, charge, first, ext, lenv, lprev)


def join_kernel(*refs):
    *pieces, out_ref, sems = refs
    copies = []
    ends = [low for low, _ in PIECES[1:]] + [PIECES[-1][1]]
    for k, (piece, (low, _), end) in enumerate(zip(pieces, PIECES, ends)):
        copies.append(
            pltpu.make_async_copy(piece.at[pl.ds(0, end - low)], out_ref.at[pl.ds(low, end - low)], sems.at[k])
        )
        copies[-1].start()
    for copy in copies:
        copy.wait()


def joined(pieces):
    _, width, _ = pieces[0].shape
    return kernel_call(
        join_kernel,
        jax.ShapeDtypeStruct((PIECES[-1][1], width, width), pieces[0].dtype),
        VMEM_SPEC,
        [pl.BlockSpec(memory_space=pl.ANY)] * len(pieces),
        "join",
        [pltpu.SemaphoreType.DMA((len(pieces),))],
    )(*pieces)


def hold_kernel(*refs):
    pass


def held_in_vmem(lenv, renv, charge, mpo):
    return pl.pallas_call(
        hold_kernel,
        out_shape=[jax.ShapeDtypeStruct(array.shape, array.dtype) for array in (lenv, renv)],
        in_specs=[VMEM_SPEC] * 2 + [SMEM_SPEC] * 2 + [pl.BlockSpec(memory_space=pl.ANY)],
        out_specs=[VMEM_SPEC] * 2,
        input_output_aliases={0: 0, 1: 1},
        name="hold",
        compiler_params=pltpu.CompilerParams(vmem_limit_bytes=VMEM_LIMIT),
    )(lenv, renv, charge, mpo, renv)


def mask_kernel(width, kept_ref, site_ref, out_ref, long_ref):
    kept = kept_ref[0]
    rows = lax.broadcasted_iota(jnp.int32, site_ref.shape, 0)
    cols = lax.broadcasted_iota(jnp.int32, site_ref.shape, 1) % width
    site = site_ref[...].astype(jnp.float32)
    site = jnp.where((rows < kept) & (cols < kept), site, 0.0).astype(jnp.bfloat16)
    fill_sent((out_ref, long_ref), site)


def masked(site, kept):
    width = site.shape[0]
    return kernel_call(
        functools.partial(mask_kernel, width),
        sent_shapes(site.shape, 0),
        [VMEM_SPEC] * 2,
        [SMEM_SPEC, VMEM_SPEC],
        "masked",
    )(kept, site)


def neighbours(x, long):
    count = lax.axis_size("blk")
    outer = lax.ppermute(long, "blk", [(i, i + 1 if i % 2 else i - 1) for i in range(1, count - 1)])
    inner = lax.ppermute(x, "blk", [(i, i ^ 1) for i in range(count)])
    return inner, outer


def passed_along(array):
    length = lax.axis_size("seg")
    return lax.ppermute(array, "seg", [(i, i + 1) for i in range(length - 1)])


def on_device(site, left_env, right_env, mpo, charge, kept):
    width = site.shape[2]
    chans = left_env.shape[1]
    peers = lax.axis_size("blk")
    factor = float(site.shape[1] * peers * width * width)
    lenv = left_env[0, :, 0]
    renv = right_env[0, :, 0]
    mpo = mpo.reshape(-1)
    limit = kept[0]
    x, long = masked(site[0, 0], limit)
    lheld, rheld = held_in_vmem(lenv, renv, charge, mpo)
    odd = (lax.axis_index("blk") % 2).astype(jnp.int32).reshape(1)
    own, inner, outer = [x], [], []
    rounded = x
    for step in range(ITERS):
        from_inner, from_outer = neighbours(rounded, long)
        inner.append(from_inner)
        outer.append(from_outer)
        if step == 0:
            from_inner, from_outer, later = lax.optimization_barrier((from_inner, from_outer, lheld))
            inner[0], outer[0] = from_inner, from_outer
            lprev = [passed_along(later[a:b]) for a, b in PIECES]
        earlier = own[:-1] if step == ITERS - 1 else []
        nxt, rounded, long, *sums = apply_ham(
            own[-1], from_inner, from_outer, lheld, rheld, mpo, charge, limit, odd, earlier, peers, step + 1
        )
        own.append(nxt)
    from_inner, from_outer = neighbours(rounded, long)
    inner.append(from_inner)
    outer.append(from_outer)
    sums = lax.all_to_all(sums[0], "blk", 0, 0)
    ext, energy = combine(own, inner, outer, sums, mpo, charge, odd, chans, width)
    arrived = passed_along(ext)
    first = (lax.axis_index("seg") == 0).astype(jnp.int32).reshape(1)
    merged = env_of(arrived, joined(lprev), lenv, mpo, charge, first, factor)
    return ext[1][None, None], energy[0, :1], merged[None, :, None]


def solution(mesh):
    placed = (
        P("seg", "blk", None, None),
        P("seg", None, "blk", None, None),
        P("seg", None, "blk", None, None),
        P(),
        P(),
        P("seg", "blk"),
    )
    return jax.shard_map(
        on_device,
        mesh=mesh,
        in_specs=placed,
        out_specs=(P("seg", "blk", None, None), P("seg"), P("seg", None, "blk", None, None)),
        check_vma=False,
    )
```
